256 devices in a mesh: sub: 16 (over y, z_lo, core), grid: 16 (over x, z_hi).
Axes of the slice: x: 4, y: 4, z: 8 (z_hi: 4, z_lo: 2; z = z_hi * 2 + z_lo), core: 2. Of those that a mesh axis runs over, the one named last changes fastest.
Arguments:
- load_parts: float32 [256, 1152, 256], P(('sub', 'grid')), may hold values from -6 to 6
- iface_len: int32 [256], P(('sub', 'grid')), may hold values from 512 to 1152
- face_rows: int32 [256, 4, 128], P(('sub', 'grid')), may hold values from 0 to 1151, as said below
- face_count: int32 [256, 4], P(('sub', 'grid')), may hold values from 0 to 128, as said below
- local_inverse: bfloat16 [256, 1152, 1152], P(('sub', 'grid')), may hold values from -0.1875 to 0.1875
- schur_offdiag: bfloat16 [256, 1152, 1152], P(('sub', 'grid')), may hold values from -0.1875 to 0.1875
- schur_diag: float32 [256, 1152], P(('sub', 'grid')), may hold values from 1 to 2
- mode_basis: bfloat16 [256, 32, 1152], P(('sub', 'grid')), may hold values from -0.1875 to 0.1875
- coarse_inverse: float32 [8192, 8192], P('grid', 'sub'), may hold values from -0.25 to 0.25
Outputs:
- solution: float32 [256, 1152, 256], P(('sub', 'grid'))
- residual: float32 [256, 1152, 256], P(('sub', 'grid'))
The draws below stay inside these ranges and needn't reach their ends.
Inputs may be any that keep to these rules, and one draw needn't show every extreme that they name: `face_rows`: each of a subdomain's 4 * 128 listed rows is below its interface length, and all are distinct. `face_count`: A face and the neighbour's opposite face have equal counts; faces at the edge of the arrangement have count 0.
All inputs are finite; a program needn't handle non-finite values.
Results may differ from the reference program's by a relative error of at most 0.0037.
Values sent between devices are 32-bit elements; how exact they have to be, the bound alone decides.
No kernel may reach another device: no remote copies, remote signals or barrier semaphores. Data moves between devices by JAX's collectives and lax.ppermute only.
A program may use at most 64 MiB of HBM per device.

```python
import jax
import jax.numpy as jnp
from jax import lax

NMAX = 1152
MODES = 32
SHARE = 128
LOADS = 256
ITERS = 2
SUBS = 256
COARSE = 8192
N_SUB = 16
N_GRID = 16


def interface_lengths(key):
    total = N_SUB * N_GRID
    lengths = jax.random.randint(jax.random.fold_in(key, 101), (total,), NMAX * 4 // 9, NMAX + 1)
    chosen = jax.random.randint(jax.random.fold_in(key, 102), (), 0, total)
    return lengths.at[chosen].set(NMAX)


def draw_iface_len(key, part):
    return interface_lengths(key).astype(jnp.int32)


def draw_face_rows(key, part):
    lengths = interface_lengths(key)
    key = jax.random.fold_in(key, 7)
    total = N_SUB * N_GRID
    noise = jax.random.randint(key, (total, NMAX), 0, 65536)
    position = jnp.arange(NMAX)
    outside = (position[None, :] >= lengths[:, None]).astype(jnp.int32)
    score = noise * NMAX + position[None, :] + outside * (65536 * NMAX)
    order = jnp.argsort(score, axis=1)
    return order[:, :4 * SHARE].reshape(total, 4, SHARE).astype(jnp.int32)


def draw_face_count(key, part):
    key = jax.random.fold_in(key, 11)
    sub_edges = jax.random.randint(jax.random.fold_in(key, 1), (N_SUB, N_GRID), SHARE // 2, SHARE + 1)
    grid_edges = jax.random.randint(jax.random.fold_in(key, 2), (N_SUB, N_GRID), SHARE // 2, SHARE + 1)
    pick_sub = jax.random.randint(jax.random.fold_in(key, 3), (), 0, N_SUB - 1)
    pick_grid = jax.random.randint(jax.random.fold_in(key, 4), (), 0, N_GRID)
    sub_edges = sub_edges.at[pick_sub, pick_grid].set(SHARE)
    sub_index = jnp.arange(N_SUB)[:, None]
    grid_index = jnp.arange(N_GRID)[None, :]
    face_zero = jnp.where(sub_index < N_SUB - 1, sub_edges, 0)
    face_one = jnp.concatenate([jnp.zeros((1, N_GRID), jnp.int32), face_zero[:-1]], axis=0)
    face_two = jnp.where(grid_index < N_GRID - 1, grid_edges, 0)
    face_three = jnp.concatenate([jnp.zeros((N_SUB, 1), jnp.int32), face_two[:, :-1]], axis=1)
    stacked = jnp.stack([face_zero, face_one, face_two, face_three], axis=-1)
    return stacked.reshape(N_SUB * N_GRID, 4).astype(jnp.int32)


def levels(own_key, dims, split, smallest, high):
    factor_of = 1.0
    for axis_at, shards_of in split:
        heights = jax.random.uniform(jax.random.fold_in(jax.random.fold_in(own_key, 6), axis_at), (shards_of,), jnp.float32, smallest / len(split), high / len(split))
        factor_of = factor_of * jnp.repeat(jnp.exp(heights), dims[axis_at] // shards_of).reshape((-1,) + (1,) * (len(dims) - 1 - axis_at))
    return factor_of


def bell_draw(rng, dims, scale, most, split=(), dtype=jnp.bfloat16):
    array = jax.random.normal(rng, dims, jnp.float32) * scale
    if len(split) > 0:
        array = levels(rng, dims, split, -0.22, 0.18) * array
    return jnp.clip(array, min=-most, max=most).astype(dtype)


def setup_inputs(seed: int = 0) -> dict:
    splits = jax.random.split(jax.random.key(seed), 10)
    load_parts = bell_draw(splits[0], (SUBS, NMAX, LOADS), 1.0, 6.0, ((0, 256),), jnp.float32)
    iface_len = draw_iface_len(jax.random.fold_in(splits[9], 71), 0)
    face_rows = draw_face_rows(jax.random.fold_in(splits[9], 71), 0)
    face_count = draw_face_count(jax.random.fold_in(splits[9], 71), 0)
    local_inverse = bell_draw(splits[4], (SUBS, NMAX, NMAX), NMAX ** -0.5, 0.1875, ((0, 256),))
    schur_offdiag = bell_draw(splits[5], (SUBS, NMAX, NMAX), NMAX ** -0.5, 0.1875, ((0, 256),))
    schur_diag = jnp.clip(1.0 + 1.0 * jax.random.uniform(splits[6], (SUBS, NMAX), jnp.float32) ** levels(splits[6], (SUBS, NMAX), ((0, 256),), -0.2, 0.2), 1.0, 2.0)
    mode_basis = bell_draw(splits[7], (SUBS, MODES, NMAX), NMAX ** -0.5, 0.1875, ((0, 256),))
    coarse_inverse = bell_draw(splits[8], (COARSE, COARSE), (MODES * N_GRID) ** -0.5, 0.25, ((0, 16), (1, 16)), jnp.float32)
    return dict(load_parts=load_parts, iface_len=iface_len, face_rows=face_rows, face_count=face_count, local_inverse=local_inverse, schur_offdiag=schur_offdiag, schur_diag=schur_diag, mode_basis=mode_basis, coarse_inverse=coarse_inverse)


def assemble(values, face_rows, face_count):
    usable = (jnp.arange(SHARE)[None, None, :] < face_count[:, :, None]).astype(jnp.float32)
    outgoing = jax.vmap(lambda vals, rows: vals[rows])(values, face_rows) * usable[..., None]
    outgoing = outgoing.reshape(N_SUB, N_GRID, 4, SHARE, LOADS)
    nothing_sub = jnp.zeros_like(outgoing[:1, :, 0])
    nothing_grid = jnp.zeros_like(outgoing[:, :1, 0])
    face_zero = jnp.concatenate([outgoing[1:, :, 1], nothing_sub], axis=0)
    face_one = jnp.concatenate([nothing_sub, outgoing[:-1, :, 0]], axis=0)
    face_two = jnp.concatenate([outgoing[:, 1:, 3], nothing_grid], axis=1)
    face_three = jnp.concatenate([nothing_grid, outgoing[:, :-1, 2]], axis=1)
    received = jnp.stack([face_zero, face_one, face_two, face_three], axis=2)
    received = received.reshape(N_SUB * N_GRID, 4 * SHARE, LOADS)
    return jax.vmap(lambda vals, rows, extra: vals.at[rows.reshape(-1)].add(extra))(values, face_rows, received)


def plain_product(pair):
    return jnp.dot(pair[0], pair[1], preferred_element_type=jnp.float32)


def spread_product(pair):
    return lax.dot_general(pair[0].astype(jnp.float32), pair[1], (((0,), (0,)), ((), ())), precision=lax.Precision.HIGHEST, preferred_element_type=jnp.float32)


def reference(load_parts, iface_len, face_rows, face_count, local_inverse, schur_offdiag, schur_diag, mode_basis, coarse_inverse):
    subs_total = N_SUB * N_GRID
    live = (jnp.arange(NMAX)[None, :] < iface_len[:, None]).astype(jnp.float32)[:, :, None]
    resid = load_parts * live
    solution = jnp.zeros_like(resid)
    for sweep in range(ITERS):
        assembled_b = assemble(resid, face_rows, face_count).astype(jnp.bfloat16)
        local_part = lax.map(plain_product, (local_inverse, assembled_b))
        coarse_in = lax.map(plain_product, (mode_basis, assembled_b))
        flat = coarse_in.reshape(subs_total * MODES, LOADS)
        coarse_out = jnp.dot(coarse_inverse, flat, precision=lax.Precision.HIGHEST)
        coarse_out = coarse_out.reshape(N_GRID, N_SUB, MODES, LOADS).transpose(1, 0, 2, 3)
        coarse_out = coarse_out.reshape(subs_total, MODES, LOADS)
        spread = lax.map(spread_product, (mode_basis, coarse_out))
        correction = live * (local_part + spread)
        increment = assemble(correction, face_rows, face_count)
        solution = solution + increment
        applied = lax.map(plain_product, (schur_offdiag, increment.astype(jnp.bfloat16)))
        applied = applied + schur_diag[:, :, None] * increment
        resid = resid - live * applied
    return solution, resid
```

```python
import functools

import jax
import jax.numpy as jnp
from jax import lax
from jax.experimental import pallas as pl
from jax.experimental.pallas import tpu as pltpu
from jax.sharding import PartitionSpec as P

ITERS = 2
VMEM_LIMIT = 32 * 1024 * 1024
F32 = jnp.float32
BF16 = jnp.bfloat16


def dot(a, b):
    return jnp.dot(a, b, preferred_element_type=F32)


def halves(v):
    high = v.astype(BF16)
    return high, (v - high.astype(F32)).astype(BF16)


def pick(onehot, v):
    high, low = halves(v)
    return dot(onehot, high) + dot(onehot, low)


def live_of(length_ref, n):
    return (lax.broadcasted_iota(jnp.int32, (n, 1), 0) < length_ref[0]).astype(F32)


def store_faces(faces, refs):
    share = refs[0].shape[0]
    for j, ref in enumerate(refs):
        ref[...] = faces[j * share : (j + 1) * share]


def load_faces(refs):
    return jnp.concatenate([ref[...] for ref in refs], axis=0)


def begin_kernel(length, rows, loads, resid, take, *faces):
    n = loads.shape[0]
    spot = lax.broadcasted_iota(jnp.int32, take.shape, 1)
    take[...] = (rows[...] == spot).astype(F32).astype(BF16)
    resid[...] = loads[...] * live_of(length, n)
    store_faces(pick(take[...], resid[...]), faces)


def tables_kernel(rows, coarse, put, coarse_high, coarse_low):
    spot = lax.broadcasted_iota(jnp.int32, put.shape, 0)
    put[...] = (rows[...] == spot).astype(F32).astype(BF16)
    high, low = halves(coarse[...])
    coarse_high[...] = high
    coarse_low[...] = low


def coarse_in_kernel(resid, f0, f1, f2, f3, put, basis, assembled, coarse_in):
    received = load_faces((f0, f1, f2, f3))
    assembled[...] = (resid[...] + pick(put[...], received)).astype(BF16)
    block = dot(basis[...], assembled[...])
    for j in range(coarse_in.shape[0]):
        coarse_in[j] = block


def local_kernel(inverse, assembled, local):
    local[...] = dot(inverse[...], assembled[...])


def coarse_kernel(core, high, low, gathered, keep, send):
    groups, modes, loads = gathered.shape
    g_high, g_low = halves(gathered[...].reshape(groups * modes, loads))
    out = dot(high[...], g_high) + dot(high[...], g_low) + dot(low[...], g_high)
    pairs = out.reshape(-1, 2, modes, loads)
    even = pairs[:, 0].reshape(keep.shape)
    odd = pairs[:, 1].reshape(keep.shape)
    first = core[0] == 0
    keep[...] = jnp.where(first, even, odd)
    send[...] = jnp.where(first, odd, even)


def correction_kernel(length, local, basis_t, parts, take, correction, *faces):
    n = local.shape[0]
    total = jnp.sum(parts[...], axis=0)
    high, low = halves(total)
    spread = dot(basis_t[...], high) + dot(basis_t[...], low)
    correction[...] = live_of(length, n) * (local[...] + spread)
    store_faces(pick(take[...], correction[...]), faces)


def increment_kernel(first, last, *refs):
    length, correction, f0, f1, f2, f3, put, offdiag, diag, resid = refs[:10]
    refs = refs[10:]
    if not first:
        before, refs = refs[0], refs[1:]
    if not last:
        take, refs = refs[0], refs[1:]
    solution_out, resid_out, *faces = refs
    n = correction.shape[0]
    increment = correction[...] + pick(put[...], load_faces((f0, f1, f2, f3)))
    solution_out[...] = increment if first else before[...] + increment
    applied = dot(offdiag[...], increment.astype(BF16)) + diag[...] * increment
    resid_out[...] = resid[...] - live_of(length, n) * applied
    if not last:
        store_faces(pick(take[...], resid_out[...]), faces)


def call(kernel, outs, args, scalars=0, flops=0):
    size = lambda a: a.size * a.dtype.itemsize
    specs = [pl.BlockSpec(memory_space=pltpu.SMEM)] * scalars
    specs += [pl.BlockSpec(memory_space=pltpu.VMEM)] * (len(args) - scalars)
    return pl.pallas_call(
        kernel,
        out_shape=outs,
        in_specs=specs,
        out_specs=[pl.BlockSpec(memory_space=pltpu.VMEM)] * len(outs),
        compiler_params=pltpu.CompilerParams(vmem_limit_bytes=VMEM_LIMIT),
        cost_estimate=pl.CostEstimate(
            flops=flops,
            bytes_accessed=sum(size(a) for a in args) + sum(size(a) for a in outs),
            transcendentals=0,
        ),
    )(*args)


def like(*shape, dtype=F32):
    return jax.ShapeDtypeStruct(shape, dtype)


def swap(array, axis, odd):
    size = lax.axis_size(axis)
    pairs = [(i, ((i + odd) ^ 1) - odd) for i in range(size)]
    return lax.ppermute(array, axis, [(i, j) for i, j in pairs if 0 <= j < size])


def exchange(faces):
    return (
        swap(faces[0], "sub", 0),
        swap(faces[1], "sub", 1),
        swap(faces[2], "grid", 0),
        swap(faces[3], "grid", 1),
    )


def body(
    load_parts,
    iface_len,
    face_rows,
    face_count,
    local_inverse,
    schur_offdiag,
    schur_diag,
    mode_basis,
    coarse_inverse,
):
    loads = load_parts[0]
    inverse = local_inverse[0]
    offdiag = schur_offdiag[0]
    diag = schur_diag[0][:, None]
    basis = mode_basis[0]
    basis_t = basis.T
    n, nloads = loads.shape
    modes = basis.shape[0]
    share = face_rows.shape[2]
    nsub = lax.axis_size("sub")
    ngrid = lax.axis_size("grid")
    core = lax.rem(lax.axis_index("sub"), 2)
    column = lax.rem(lax.axis_index("grid"), 2)

    usable = jnp.arange(share)[None, :] < face_count[0][:, None]
    rows = jnp.where(usable, face_rows[0], -1)
    rows_sub = jnp.where(core == 0, rows[:2], rows[1::-1])
    rows_grid = jnp.where(column == 0, rows[2:], rows[:1:-1])
    rows = jnp.concatenate([rows_sub, rows_grid], axis=0).reshape(-1)
    nrows = rows.shape[0]
    core = core[None]

    face = like(share, nloads)
    block = like(n, nloads)
    gather_flops = 4 * nrows * n * nloads
    square_flops = 2 * n * n * nloads

    resid, take, *faces = call(
        begin_kernel,
        [block, like(nrows, n, dtype=BF16)] + [face] * 4,
        (iface_len, rows[:, None], loads),
        scalars=1,
        flops=gather_flops,
    )
    order = coarse_inverse.shape
    put, coarse_high, coarse_low = call(
        tables_kernel,
        [like(n, nrows, dtype=BF16), like(*order, dtype=BF16), like(*order, dtype=BF16)],
        (rows[None, :], coarse_inverse),
    )
    solution = None
    for sweep in range(ITERS):
        first, last = sweep == 0, sweep == ITERS - 1
        received = exchange(faces)
        assembled, coarse_in = call(
            coarse_in_kernel,
            [like(n, nloads, dtype=BF16), like(ngrid, modes, nloads)],
            (resid, *received, put, basis),
            flops=gather_flops,
        )
        gathered = lax.all_to_all(coarse_in, "grid", 0, 0)
        keep, send = call(
            coarse_kernel,
            [like(order[0] // 2, nloads)] * 2,
            (core, coarse_high, coarse_low, gathered),
            scalars=1,
            flops=6 * order[0] * order[1] * nloads,
        )
        other = swap(send, "sub", 0)
        (local,) = call(local_kernel, [block], (inverse, assembled), flops=square_flops)
        parts = (keep + other).reshape(nsub // 2, modes, nloads)
        groups = [list(range(i, nsub, 2)) for i in range(2)]
        parts = lax.all_to_all(parts, "sub", 0, 0, axis_index_groups=groups)
        correction, *faces = call(
            correction_kernel,
            [block] + [face] * 4,
            (iface_len, local, basis_t, parts, take),
            scalars=1,
            flops=gather_flops,
        )
        received = exchange(faces)
        args = (iface_len, correction, *received, put, offdiag, diag, resid)
        args += () if first else (solution,)
        args += () if last else (take,)
        solution, resid, *faces = call(
            functools.partial(increment_kernel, first, last),
            [block, block] + ([] if last else [face] * 4),
            args,
            scalars=1,
            flops=square_flops + gather_flops * (1 if last else 2),
        )
    return (solution[None], resid[None])


def solution(mesh):
    in_specs = (
        P(("sub", "grid"), None, None),
        P(("sub", "grid")),
        P(("sub", "grid"), None, None),
        P(("sub", "grid"), None),
        P(("sub", "grid"), None, None),
        P(("sub", "grid"), None, None),
        P(("sub", "grid"), None),
        P(("sub", "grid"), None, None),
        P("grid", "sub"),
    )
    out_specs = (P(("sub", "grid"), None, None), P(("sub", "grid"), None, None))
    return jax.shard_map(body, mesh=mesh, in_specs=in_specs, out_specs=out_specs, check_vma=False)
```

```python
import jax
import jax.numpy as jnp
from jax import lax
from jax.experimental import pallas as pl
from jax.experimental.pallas import tpu as pltpu
from jax.sharding import PartitionSpec as P

ITERS = 2
CHUNKS = 4
VMEM_LIMIT = 32 * 1024 * 1024
F32 = jnp.float32
BF16 = jnp.bfloat16


def dot(a, b):
    return jnp.dot(a, b, preferred_element_type=F32)


def halves(v):
    high = v.astype(BF16)
    return high, (v - high.astype(F32)).astype(BF16)


def pick(onehot, v):
    high, low = halves(v)
    return dot(onehot, high) + dot(onehot, low)


def live_of(length_ref, n):
    return (lax.broadcasted_iota(jnp.int32, (n, 1), 0) < length_ref[0]).astype(F32)


def onehot(rows, shape, axis):
    spot = lax.broadcasted_iota(jnp.int32, shape, axis)
    return (rows == spot).astype(F32).astype(BF16)


def store_faces(faces, refs):
    share = refs[0].shape[0]
    for j, ref in enumerate(refs):
        ref[...] = faces[j * share : (j + 1) * share]


def load_faces(refs):
    return jnp.concatenate([ref[...] for ref in refs], axis=0)


def chunks(n):
    return [slice(j * (n // CHUNKS), (j + 1) * (n // CHUNKS)) for j in range(CHUNKS)]


def chunk_copies(source, target, sems):
    return [
        pltpu.make_async_copy(source.at[part], target.at[part], sems.at[j])
        for j, part in enumerate(chunks(target.shape[0]))
    ]


def begin_kernel(length, rows, loads, resid, take, f0, f1, f2, f3, sems):
    n = resid.shape[0]
    copies = chunk_copies(loads, resid, sems)
    for copy in copies:
        copy.start()
    take[...] = onehot(rows[...], take.shape, 1)
    for copy in copies:
        copy.wait()
    resid[...] = resid[...] * live_of(length, n)
    store_faces(pick(take[...], resid[...]), (f0, f1, f2, f3))


def tables_kernel(rows, coarse, put, coarse_high, coarse_low):
    put[...] = onehot(rows[...], put.shape, 0)
    high, low = halves(coarse[...])
    coarse_high[...] = high
    coarse_low[...] = low


def coarse_in_kernel(resid, f0, f1, f2, f3, put, basis, assembled, coarse_in, token):
    token[...] = jnp.zeros_like(token)
    received = load_faces((f0, f1, f2, f3))
    assembled[...] = (resid[...] + pick(put[...], received)).astype(BF16)
    block = dot(basis[...], assembled[...])
    for j in range(coarse_in.shape[0]):
        coarse_in[j] = block


def local_kernel(inverse, assembled, take, local, local_faces, token):
    local[...] = dot(inverse[...], assembled[...])
    local_faces[...] = pick(take[...], local[...])
    token[...] = jnp.zeros_like(token)


def coarse_kernel(core, high, low, gathered, after, after_too, keep, send):
    groups, modes, loads = gathered.shape
    g_high, g_low = halves(gathered[...].reshape(groups * modes, loads))
    out = dot(high[...], g_high) + dot(high[...], g_low) + dot(low[...], g_high)
    pairs = out.reshape(-1, 2, modes, loads)
    even = pairs[:, 0].reshape(keep.shape)
    odd = pairs[:, 1].reshape(keep.shape)
    first = core[0] == 0
    keep[...] = jnp.where(first, even, odd)
    send[...] = jnp.where(first, odd, even)


def rows_kernel(after, take, offdiag, basis_t, diag_row, offdiag_rows, basis_rows, diag_rows, token):
    token[...] = after[...]
    basis_rows[...] = dot(take[...], basis_t[...]).astype(BF16)
    diag_rows[...] = jnp.sum(take[...].astype(F32) * diag_row[...], axis=1, keepdims=True)
    offdiag_rows[...] = dot(take[...], offdiag[...]).astype(BF16)


def columns_kernel(after, offdiag, put, offdiag_columns, token):
    token[...] = after[...]
    offdiag_columns[...] = dot(offdiag[...], put[...]).astype(BF16)


def sent_kernel(parts, local_faces, basis_rows, coarse_out, f0, f1, f2, f3):
    total = jnp.sum(parts[...], axis=0)
    coarse_out[...] = total
    high, low = halves(total)
    rows = basis_rows[...]
    store_faces(local_faces[...] + dot(rows, high) + dot(rows, low), (f0, f1, f2, f3))


def correct(length, local, basis_t, coarse_out):
    high, low = halves(coarse_out[...])
    spread = dot(basis_t[...], high) + dot(basis_t[...], low)
    return live_of(length, local.shape[0]) * (local[...] + spread)


def correction_kernel(length, local, basis_t, coarse_out, correction):
    correction[...] = correct(length, local, basis_t, coarse_out)


def increment_kernel(correction, r0, r1, r2, r3, put, offdiag_rows, diag_rows, c0, c1, c2, c3, p0, p1, p2, p3,
                     increment, g0, g1, g2, g3):
    received = load_faces((r0, r1, r2, r3))
    increment[...] = correction[...] + pick(put[...], received)
    there = load_faces((c0, c1, c2, c3)) + received
    applied = dot(offdiag_rows[...], increment[...].astype(BF16)) + diag_rows[...] * there
    store_faces(load_faces((p0, p1, p2, p3)) - applied, (g0, g1, g2, g3))


def residual_kernel(length, increment, diag, resid, offdiag, resid_out):
    applied = dot(offdiag[...], increment[...].astype(BF16)) + diag[...] * increment[...]
    resid_out[...] = resid[...] - live_of(length, resid.shape[0]) * applied


def own_kernel(length, local, basis_t, coarse_out, before, diag, resid, offdiag,
               solution, resid_out):
    correction = correct(length, local, basis_t, coarse_out)
    solution[...] = before[...] + correction
    applied = dot(offdiag[...], correction.astype(BF16)) + diag[...] * correction
    resid_out[...] = resid[...] - live_of(length, resid.shape[0]) * applied


def finish_kernel(length, r0, r1, r2, r3, put, offdiag_columns, diag, own, own_resid,
                  solution, resid_out, total, rest, total_sems, rest_sems):
    n = own.shape[0]
    totals = chunk_copies(total, solution, total_sems)
    rests = chunk_copies(rest, resid_out, rest_sems)
    high, low = halves(load_faces((r0, r1, r2, r3)))
    live = live_of(length, n)
    for part, leave, leave_too in zip(chunks(n), totals, rests):
        added = dot(put[part], high) + dot(put[part], low)
        total[part] = own[part] + added
        leave.start()
        applied = dot(offdiag_columns[part], high) + diag[part] * added
        rest[part] = own_resid[part] - live[part] * applied
        leave_too.start()
    for copy in totals + rests:
        copy.wait()


def call(kernel, outs, args, places, out_places="", scratch=(), flops=0):
    size = lambda a: a.size * a.dtype.itemsize
    kinds = dict(s=pltpu.SMEM, v=pltpu.VMEM, h=pltpu.HBM)
    out_places = out_places or "v" * len(outs)
    return pl.pallas_call(
        kernel,
        out_shape=outs,
        in_specs=[pl.BlockSpec(memory_space=kinds[c]) for c in places],
        out_specs=[pl.BlockSpec(memory_space=kinds[c]) for c in out_places],
        scratch_shapes=list(scratch),
        compiler_params=pltpu.CompilerParams(vmem_limit_bytes=VMEM_LIMIT),
        cost_estimate=pl.CostEstimate(
            flops=flops,
            bytes_accessed=sum(size(a) for a in args) + sum(size(a) for a in outs),
            transcendentals=0,
        ),
    )(*args)


def like(*shape, dtype=F32):
    return jax.ShapeDtypeStruct(shape, dtype)


def swap(array, axis, odd):
    size = lax.axis_size(axis)
    pairs = [(i, ((i + odd) ^ 1) - odd) for i in range(size)]
    return lax.ppermute(array, axis, [(i, j) for i, j in pairs if 0 <= j < size])


def exchange(faces):
    return (
        swap(faces[0], "grid", 0),
        swap(faces[1], "grid", 1),
        swap(faces[2], "sub", 1),
        swap(faces[3], "sub", 0),
    )


def body(
    load_parts,
    iface_len,
    face_rows,
    face_count,
    local_inverse,
    schur_offdiag,
    schur_diag,
    mode_basis,
    coarse_inverse,
):
    loads = load_parts[0]
    inverse = local_inverse[0]
    offdiag = schur_offdiag[0]
    diag = schur_diag[0][:, None]
    basis = mode_basis[0]
    basis_t = basis.T
    n, nloads = loads.shape
    modes = basis.shape[0]
    share = face_rows.shape[2]
    nsub = lax.axis_size("sub")
    ngrid = lax.axis_size("grid")
    core = lax.rem(lax.axis_index("sub"), 2)
    column = lax.rem(lax.axis_index("grid"), 2)

    usable = jnp.arange(share)[None, :] < face_count[0][:, None]
    rows = jnp.where(usable, face_rows[0], -1)
    rows_grid = jnp.where(column == 0, rows[2:], rows[:1:-1])
    rows_sub = jnp.where(core == 0, rows[1::-1], rows[:2])
    rows = jnp.concatenate([rows_grid, rows_sub], axis=0).reshape(-1)
    nrows = rows.shape[0]
    core = core[None]

    face = like(share, nloads)
    block = like(n, nloads)
    gather_flops = 4 * nrows * n * nloads
    square_flops = 2 * n * n * nloads

    order = coarse_inverse.shape
    sems = pltpu.SemaphoreType.DMA((CHUNKS,))
    mark = like(8, 128)
    resid, take, *sent = call(
        begin_kernel,
        [block, like(nrows, n, dtype=BF16)] + [face] * 4,
        (iface_len, rows[:, None], loads),
        "svh",
        scratch=[sems],
        flops=gather_flops,
    )
    put, coarse_high, coarse_low = call(
        tables_kernel,
        [like(n, nrows, dtype=BF16), like(*order, dtype=BF16), like(*order, dtype=BF16)],
        (rows[None, :], coarse_inverse),
        "vv",
    )
    solution = None
    for sweep in range(ITERS):
        received = exchange(sent)
        assembled, coarse_in, after = call(
            coarse_in_kernel,
            [like(n, nloads, dtype=BF16), like(ngrid, modes, nloads), mark],
            (resid, *received, put, basis),
            "v" * 7,
            flops=gather_flops,
        )
        gathered = lax.all_to_all(coarse_in, "grid", 0, 0)
        local, local_faces, ahead = call(
            local_kernel,
            [block, like(nrows, nloads), mark],
            (inverse, assembled, take),
            "vvv",
            flops=square_flops + gather_flops,
        )
        if sweep == 0:
            offdiag_rows, basis_rows, diag_rows, ahead_too = call(
                rows_kernel,
                [like(nrows, n, dtype=BF16), like(nrows, modes, dtype=BF16), like(nrows, 1), mark],
                (after, take, offdiag, basis_t, schur_diag),
                "vvvvv",
                flops=2 * nrows * n * n,
            )
        else:
            offdiag_columns, ahead_too = call(
                columns_kernel,
                [like(n, nrows, dtype=BF16), mark],
                (after, offdiag, put),
                "vvv",
                flops=2 * nrows * n * n,
            )
        keep, send = call(
            coarse_kernel,
            [like(order[0] // 2, nloads)] * 2,
            (core, coarse_high, coarse_low, gathered, ahead, ahead_too),
            "svvvvv",
            flops=6 * order[0] * order[1] * nloads,
        )
        other = swap(send, "sub", 0)
        parts = (keep + other).reshape(nsub // 2, modes, nloads)
        groups = [list(range(i, nsub, 2)) for i in range(2)]
        parts = lax.all_to_all(parts, "sub", 0, 0, axis_index_groups=groups)
        coarse_out, *corrected = call(
            sent_kernel,
            [like(modes, nloads)] + [face] * 4,
            (parts, local_faces, basis_rows),
            "vvv",
        )
        received = exchange(corrected)
        if sweep < ITERS - 1:
            (correction,) = call(
                correction_kernel, [block], (iface_len, local, basis_t, coarse_out), "svvv"
            )
            increment, *sent = call(
                increment_kernel,
                [block] + [face] * 4,
                (correction, *received, put, offdiag_rows, diag_rows, *corrected, *sent),
                "v" * 16,
                flops=2 * gather_flops,
            )
            (resid,) = call(
                residual_kernel,
                [block],
                (iface_len, increment, diag, resid, offdiag),
                "svvvv",
                flops=square_flops,
            )
            solution = increment if solution is None else solution + increment
        else:
            own, own_resid = call(
                own_kernel,
                [block, block],
                (iface_len, local, basis_t, coarse_out, solution, diag, resid, offdiag),
                "svvvvvvv",
                flops=square_flops,
            )
            solution, resid = call(
                finish_kernel,
                [block, block],
                (iface_len, *received, put, offdiag_columns, diag, own, own_resid),
                "s" + "v" * 9,
                "hh",
                [pltpu.VMEM((n, nloads), F32)] * 2 + [sems] * 2,
                flops=2 * gather_flops,
            )
    return (solution[None], resid[None])


def solution(mesh):
    in_specs = (
        P(("sub", "grid"), None, None),
        P(("sub", "grid")),
        P(("sub", "grid"), None, None),
        P(("sub", "grid"), None),
        P(("sub", "grid"), None, None),
        P(("sub", "grid"), None, None),
        P(("sub", "grid"), None),
        P(("sub", "grid"), None, None),
        P("grid", "sub"),
    )
    out_specs = (P(("sub", "grid"), None, None), P(("sub", "grid"), None, None))
    return jax.shard_map(body, mesh=mesh, in_specs=in_specs, out_specs=out_specs, check_vma=False)
```

```python
import jax
import jax.numpy as jnp
from jax import lax
from jax.experimental import pallas as pl
from jax.experimental.pallas import tpu as pltpu
from jax.sharding import PartitionSpec as P

ITERS = 2
CHUNKS = 4
VMEM_LIMIT = 32 * 1024 * 1024
F32 = jnp.float32
BF16 = jnp.bfloat16


def dot(a, b):
    return jnp.dot(a, b, preferred_element_type=F32)


def halves(v):
    high = v.astype(BF16)
    return high, (v - high.astype(F32)).astype(BF16)


def dot_t(a, b):
    return lax.dot_general(a, b, (((0,), (0,)), ((), ())), preferred_element_type=F32)


def place(put, v):
    high, low = halves(v)
    return dot(put, high) + dot(put, low)


def take(put, v):
    high, low = halves(v)
    return dot_t(put, high) + dot_t(put, low)


def live_of(length_ref, n):
    return (lax.broadcasted_iota(jnp.int32, (n, 1), 0) < length_ref[0]).astype(F32)


def onehot(rows, shape, axis):
    spot = lax.broadcasted_iota(jnp.int32, shape, axis)
    return (rows == spot).astype(F32).astype(BF16)


def store_faces(faces, refs):
    share = refs[0].shape[0]
    for j, ref in enumerate(refs):
        ref[...] = faces[j * share : (j + 1) * share]


def load_faces(refs):
    return jnp.concatenate([ref[...] for ref in refs], axis=0)


def chunks(n):
    return [slice(j * (n // CHUNKS), (j + 1) * (n // CHUNKS)) for j in range(CHUNKS)]


def chunk_copies(source, target, sems):
    return [
        pltpu.make_async_copy(source.at[part], target.at[part], sems.at[j])
        for j, part in enumerate(chunks(target.shape[0]))
    ]


def put_kernel(rows, put):
    put[...] = onehot(rows[...], put.shape, 0)


def begin_kernel(length, loads, put, resid, f0, f1, f2, f3):
    resid[...] = loads[...] * live_of(length, resid.shape[0])
    store_faces(take(put[...], resid[...]), (f0, f1, f2, f3))


def coarse_in_kernel(resid, f0, f1, f2, f3, put, basis, assembled, coarse_in, token):
    token[...] = jnp.zeros_like(token)
    received = load_faces((f0, f1, f2, f3))
    assembled[...] = (resid[...] + place(put[...], received)).astype(BF16)
    block = dot(basis[...], assembled[...])
    for j in range(coarse_in.shape[0]):
        coarse_in[j] = block


def local_kernel(inverse, assembled, put, local, local_faces, token):
    local[...] = dot(inverse[...], assembled[...])
    local_faces[...] = take(put[...], local[...])
    token[...] = jnp.zeros_like(token)


def coarse_kernel(core, coarse, gathered, after, after_too, keep, send):
    groups, modes, loads = gathered.shape
    g_high, g_low = halves(gathered[...].reshape(groups * modes, loads))
    high, low = halves(coarse[...])
    out = dot(high, g_high) + dot(high, g_low) + dot(low, g_high)
    pairs = out.reshape(-1, 2, modes, loads)
    even = pairs[:, 0].reshape(keep.shape)
    odd = pairs[:, 1].reshape(keep.shape)
    first = core[0] == 0
    keep[...] = jnp.where(first, even, odd)
    send[...] = jnp.where(first, odd, even)


def rows_kernel(after, put, offdiag, basis_t, diag, offdiag_rows, basis_rows, diag_rows, token):
    token[...] = after[...]
    basis_rows[...] = dot_t(put[...], basis_t[...]).astype(BF16)
    wide = jnp.broadcast_to(diag[...], (diag.shape[0], 128))
    diag_rows[...] = take(put[...], wide)
    offdiag_rows[...] = dot_t(put[...], offdiag[...]).astype(BF16)


def sent_kernel(parts, local_faces, basis_rows, coarse_out, f0, f1, f2, f3):
    total = jnp.sum(parts[...], axis=0)
    coarse_out[...] = total
    high, low = halves(total)
    rows = basis_rows[...]
    store_faces(local_faces[...] + dot(rows, high) + dot(rows, low), (f0, f1, f2, f3))


def correct(length, local, basis_t, coarse_out):
    high, low = halves(coarse_out[...])
    spread = dot(basis_t[...], high) + dot(basis_t[...], low)
    return live_of(length, local.shape[0]) * (local[...] + spread)


def correction_kernel(length, local, basis_t, coarse_out, correction):
    correction[...] = correct(length, local, basis_t, coarse_out)


def increment_kernel(correction, r0, r1, r2, r3, put, offdiag_rows, diag_rows, c0, c1, c2, c3, p0, p1, p2, p3,
                     increment, g0, g1, g2, g3):
    received = load_faces((r0, r1, r2, r3))
    increment[...] = correction[...] + place(put[...], received)
    there = load_faces((c0, c1, c2, c3)) + received
    applied = dot(offdiag_rows[...], increment[...].astype(BF16)) + diag_rows[:, :1] * there
    store_faces(load_faces((p0, p1, p2, p3)) - applied, (g0, g1, g2, g3))


def residual_kernel(length, increment, diag, resid, offdiag, put, resid_out, solution, offdiag_columns, sem):
    leave = pltpu.make_async_copy(increment, solution, sem)
    leave.start()
    applied = dot(offdiag[...], increment[...].astype(BF16)) + diag[...] * increment[...]
    resid_out[...] = resid[...] - live_of(length, resid.shape[0]) * applied
    offdiag_columns[...] = dot(offdiag[...], put[...]).astype(BF16)
    leave.wait()


def own_kernel(length, local, basis_t, coarse_out, before, diag, resid, offdiag,
               solution, resid_out):
    correction = correct(length, local, basis_t, coarse_out)
    solution[...] = before[...] + correction
    applied = dot(offdiag[...], correction.astype(BF16)) + diag[...] * correction
    resid_out[...] = resid[...] - live_of(length, resid.shape[0]) * applied


def finish_kernel(length, r0, r1, r2, r3, put, offdiag_columns, diag, own, own_resid,
                  solution, resid_out, total, rest, total_sems, rest_sems):
    n = own.shape[0]
    totals = chunk_copies(total, solution, total_sems)
    rests = chunk_copies(rest, resid_out, rest_sems)
    high, low = halves(load_faces((r0, r1, r2, r3)))
    live = live_of(length, n)
    for part, leave, leave_too in zip(chunks(n), totals, rests):
        added = dot(put[part], high) + dot(put[part], low)
        total[part] = own[part] + added
        leave.start()
        applied = dot(offdiag_columns[part], high) + diag[part] * added
        rest[part] = own_resid[part] - live[part] * applied
        leave_too.start()
    for copy in totals + rests:
        copy.wait()


def call(kernel, outs, args, places, out_places="", scratch=(), flops=0):
    size = lambda a: a.size * a.dtype.itemsize
    kinds = dict(s=pltpu.SMEM, v=pltpu.VMEM, h=pltpu.HBM)
    out_places = out_places or "v" * len(outs)
    return pl.pallas_call(
        kernel,
        out_shape=outs,
        in_specs=[pl.BlockSpec(memory_space=kinds[c]) for c in places],
        out_specs=[pl.BlockSpec(memory_space=kinds[c]) for c in out_places],
        scratch_shapes=list(scratch),
        compiler_params=pltpu.CompilerParams(vmem_limit_bytes=VMEM_LIMIT),
        cost_estimate=pl.CostEstimate(
            flops=flops,
            bytes_accessed=sum(size(a) for a in args) + sum(size(a) for a in outs),
            transcendentals=0,
        ),
    )(*args)


def like(*shape, dtype=F32):
    return jax.ShapeDtypeStruct(shape, dtype)


def swap(array, axis, odd):
    size = lax.axis_size(axis)
    pairs = [(i, ((i + odd) ^ 1) - odd) for i in range(size)]
    return lax.ppermute(array, axis, [(i, j) for i, j in pairs if 0 <= j < size])


def exchange(faces):
    return (
        swap(faces[0], "grid", 0),
        swap(faces[1], "grid", 1),
        swap(faces[2], "sub", 1),
        swap(faces[3], "sub", 0),
    )


def body(
    load_parts,
    iface_len,
    face_rows,
    face_count,
    local_inverse,
    schur_offdiag,
    schur_diag,
    mode_basis,
    coarse_inverse,
):
    loads = load_parts[0]
    inverse = local_inverse[0]
    offdiag = schur_offdiag[0]
    diag = schur_diag[0][:, None]
    basis = mode_basis[0]
    basis_t = basis.T
    n, nloads = loads.shape
    modes = basis.shape[0]
    share = face_rows.shape[2]
    nsub = lax.axis_size("sub")
    ngrid = lax.axis_size("grid")
    core = lax.rem(lax.axis_index("sub"), 2)
    column = lax.rem(lax.axis_index("grid"), 2)

    usable = jnp.arange(share)[None, :] < face_count[0][:, None]
    rows = jnp.where(usable, face_rows[0], -1)
    rows_grid = jnp.where(column == 0, rows[2:], rows[:1:-1])
    rows_sub = jnp.where(core == 0, rows[1::-1], rows[:2])
    rows = jnp.concatenate([rows_grid, rows_sub], axis=0).reshape(-1)
    nrows = rows.shape[0]
    core = core[None]

    face = like(share, nloads)
    block = like(n, nloads)
    gather_flops = 4 * nrows * n * nloads
    square_flops = 2 * n * n * nloads

    order = coarse_inverse.shape
    sems = pltpu.SemaphoreType.DMA((CHUNKS,))
    mark = like(8, 128)
    (put,) = call(put_kernel, [like(n, nrows, dtype=BF16)], (rows[None, :],), "v")
    resid, *sent = call(
        begin_kernel, [block] + [face] * 4, (iface_len, loads, put), "svv", flops=gather_flops
    )
    solution = None
    for sweep in range(ITERS):
        received = exchange(sent)
        assembled, coarse_in, after = call(
            coarse_in_kernel,
            [like(n, nloads, dtype=BF16), like(ngrid, modes, nloads), mark],
            (resid, *received, put, basis),
            "v" * 7,
            flops=gather_flops,
        )
        gathered = lax.all_to_all(coarse_in, "grid", 0, 0)
        local, local_faces, ahead = call(
            local_kernel,
            [block, like(nrows, nloads), mark],
            (inverse, assembled, put),
            "vvv",
            flops=square_flops + gather_flops,
        )
        if sweep == 0:
            offdiag_rows, basis_rows, diag_rows, ahead_too = call(
                rows_kernel,
                [like(nrows, n, dtype=BF16), like(nrows, modes, dtype=BF16), like(nrows, 128), mark],
                (after, put, offdiag, basis_t, diag),
                "vvvvv",
                flops=2 * nrows * n * n,
            )
        keep, send = call(
            coarse_kernel,
            [like(order[0] // 2, nloads)] * 2,
            (core, coarse_inverse, gathered, ahead, ahead_too),
            "svvvv",
            flops=6 * order[0] * order[1] * nloads,
        )
        other = swap(send, "sub", 0)
        parts = (keep + other).reshape(nsub // 2, modes, nloads)
        groups = [list(range(i, nsub, 2)) for i in range(2)]
        parts = lax.all_to_all(parts, "sub", 0, 0, axis_index_groups=groups)
        coarse_out, *corrected = call(
            sent_kernel,
            [like(modes, nloads)] + [face] * 4,
            (parts, local_faces, basis_rows),
            "vvv",
        )
        received = exchange(corrected)
        if sweep < ITERS - 1:
            (correction,) = call(
                correction_kernel, [block], (iface_len, local, basis_t, coarse_out), "svvv"
            )
            increment, *sent = call(
                increment_kernel,
                [block] + [face] * 4,
                (correction, *received, put, offdiag_rows, diag_rows, *corrected, *sent),
                "v" * 16,
                flops=2 * gather_flops,
            )
            assert solution is None
            resid, solution, offdiag_columns = call(
                residual_kernel,
                [block, block, like(n, nrows, dtype=BF16)],
                (iface_len, increment, diag, resid, offdiag, put),
                "svvvvv",
                "vhv",
                [pltpu.SemaphoreType.DMA],
                flops=square_flops,
            )
        else:
            own, own_resid = call(
                own_kernel,
                [block, block],
                (iface_len, local, basis_t, coarse_out, solution, diag, resid, offdiag),
                "svvvvvvv",
                flops=square_flops,
            )
            solution, resid = call(
                finish_kernel,
                [block, block],
                (iface_len, *received, put, offdiag_columns, diag, own, own_resid),
                "s" + "v" * 9,
                "hh",
                [pltpu.VMEM((n, nloads), F32)] * 2 + [sems] * 2,
                flops=2 * gather_flops,
            )
    return (solution[None], resid[None])


def solution(mesh):
    in_specs = (
        P(("sub", "grid"), None, None),
        P(("sub", "grid")),
        P(("sub", "grid"), None, None),
        P(("sub", "grid"), None),
        P(("sub", "grid"), None, None),
        P(("sub", "grid"), None, None),
        P(("sub", "grid"), None),
        P(("sub", "grid"), None, None),
        P("grid", "sub"),
    )
    out_specs = (P(("sub", "grid"), None, None), P(("sub", "grid"), None, None))
    return jax.shard_map(body, mesh=mesh, in_specs=in_specs, out_specs=out_specs, check_vma=False)
```

```python
import jax
import jax.numpy as jnp
from jax import lax
from jax.experimental import pallas as pl
from jax.experimental.pallas import tpu as pltpu
from jax.sharding import PartitionSpec as P

ITERS = 2
CHUNKS = 4
VMEM_LIMIT = 32 * 1024 * 1024
F32 = jnp.float32
BF16 = jnp.bfloat16


def dot(a, b):
    return jnp.dot(a, b, preferred_element_type=F32)


def halves(v):
    high = v.astype(BF16)
    return high, (v - high.astype(F32)).astype(BF16)


def dot_t(a, b):
    return lax.dot_general(a, b, (((0,), (0,)), ((), ())), preferred_element_type=F32)


def place(put, v):
    high, low = halves(v)
    return dot(put, high) + dot(put, low)


def take(put, v):
    high, low = halves(v)
    return dot_t(put, high) + dot_t(put, low)


def live_of(length_ref, n):
    return (lax.broadcasted_iota(jnp.int32, (n, 1), 0) < length_ref[0]).astype(F32)


def onehot(rows, shape, axis):
    spot = lax.broadcasted_iota(jnp.int32, shape, axis)
    return (rows == spot).astype(F32).astype(BF16)


def store_faces(faces, refs):
    share = refs[0].shape[0]
    for j, ref in enumerate(refs):
        ref[...] = faces[j * share : (j + 1) * share]


def load_faces(refs):
    return jnp.concatenate([ref[...] for ref in refs], axis=0)


def chunks(n):
    return [slice(j * (n // CHUNKS), (j + 1) * (n // CHUNKS)) for j in range(CHUNKS)]


def chunk_copies(source, target, sems):
    return [
        pltpu.make_async_copy(source.at[part], target.at[part], sems.at[j])
        for j, part in enumerate(chunks(target.shape[0]))
    ]


def put_kernel(rows, put):
    put[...] = onehot(rows[...], put.shape, 0)


def begin_kernel(length, loads, put, resid, f0, f1, f2, f3):
    resid[...] = loads[...] * live_of(length, resid.shape[0])
    store_faces(take(put[...], resid[...]), (f0, f1, f2, f3))


def coarse_in_kernel(resid, f0, f1, f2, f3, put, basis, assembled, coarse_in, token):
    token[...] = jnp.zeros_like(token)
    received = load_faces((f0, f1, f2, f3))
    assembled[...] = (resid[...] + place(put[...], received)).astype(BF16)
    block = dot(basis[...], assembled[...])
    for j in range(coarse_in.shape[0]):
        coarse_in[j] = block


def local_kernel(inverse, assembled, put, local, local_faces, token):
    local[...] = dot(inverse[...], assembled[...])
    local_faces[...] = take(put[...], local[...])
    token[...] = jnp.zeros_like(token)


def late_local_kernel(after, inverse, assembled, local, token):
    token[...] = after[...]
    local[...] = dot(inverse[...], assembled[...])


def sum_kernel(keep, other, after, out):
    out[...] = (keep[...] + other[...]).reshape(out.shape)


def coarse_kernel(core, coarse, gathered, after, after_too, keep, send, token):
    token[...] = after[...]
    groups, modes, loads = gathered.shape
    g_high, g_low = halves(gathered[...].reshape(groups * modes, loads))
    high, low = halves(coarse[...])
    out = dot(high, g_high) + dot(high, g_low) + dot(low, g_high)
    pairs = out.reshape(-1, 2, modes, loads)
    even = pairs[:, 0].reshape(keep.shape)
    odd = pairs[:, 1].reshape(keep.shape)
    first = core[0] == 0
    keep[...] = jnp.where(first, even, odd)
    send[...] = jnp.where(first, odd, even)


def rows_kernel(after, put, offdiag, basis_t, diag, offdiag_rows, basis_rows, diag_rows, token):
    token[...] = after[...]
    basis_rows[...] = dot_t(put[...], basis_t[...]).astype(BF16)
    wide = jnp.broadcast_to(diag[...], (diag.shape[0], 128))
    diag_rows[...] = take(put[...], wide)
    offdiag_rows[...] = dot_t(put[...], offdiag[...]).astype(BF16)


def late_sent_kernel(parts, local, put, basis_rows, coarse_out, f0, f1, f2, f3):
    total = jnp.sum(parts[...], axis=0)
    coarse_out[...] = total
    high, low = halves(total)
    rows = basis_rows[...]
    store_faces(take(put[...], local[...]) + dot(rows, high) + dot(rows, low), (f0, f1, f2, f3))


def sent_kernel(parts, local_faces, basis_rows, coarse_out, f0, f1, f2, f3):
    total = jnp.sum(parts[...], axis=0)
    coarse_out[...] = total
    high, low = halves(total)
    rows = basis_rows[...]
    store_faces(local_faces[...] + dot(rows, high) + dot(rows, low), (f0, f1, f2, f3))


def correct(length, local, basis_t, coarse_out):
    high, low = halves(coarse_out[...])
    spread = dot(basis_t[...], high) + dot(basis_t[...], low)
    return live_of(length, local.shape[0]) * (local[...] + spread)


def correction_kernel(length, local, basis_t, coarse_out, correction):
    correction[...] = correct(length, local, basis_t, coarse_out)


def increment_kernel(correction, r0, r1, r2, r3, put, offdiag_rows, diag_rows, c0, c1, c2, c3, p0, p1, p2, p3,
                     increment, g0, g1, g2, g3):
    received = load_faces((r0, r1, r2, r3))
    increment[...] = correction[...] + place(put[...], received)
    there = load_faces((c0, c1, c2, c3)) + received
    applied = dot(offdiag_rows[...], increment[...].astype(BF16)) + diag_rows[:, :1] * there
    store_faces(load_faces((p0, p1, p2, p3)) - applied, (g0, g1, g2, g3))


def residual_kernel(length, increment, diag, loads, offdiag, put, resid_out, solution, offdiag_columns, sem):
    leave = pltpu.make_async_copy(increment, solution, sem)
    leave.start()
    applied = dot(offdiag[...], increment[...].astype(BF16)) + diag[...] * increment[...]
    resid_out[...] = (loads[...] - applied) * live_of(length, loads.shape[0])
    offdiag_columns[...] = dot(offdiag[...], put[...]).astype(BF16)
    leave.wait()


def own_kernel(length, local, basis_t, coarse_out, before, diag, resid, offdiag,
               solution, resid_out):
    correction = correct(length, local, basis_t, coarse_out)
    solution[...] = before[...] + correction
    applied = dot(offdiag[...], correction.astype(BF16)) + diag[...] * correction
    resid_out[...] = resid[...] - live_of(length, resid.shape[0]) * applied


def finish_kernel(length, r0, r1, r2, r3, put, offdiag_columns, diag, own, own_resid,
                  solution, resid_out, total, rest, total_sems, rest_sems):
    n = own.shape[0]
    totals = chunk_copies(total, solution, total_sems)
    rests = chunk_copies(rest, resid_out, rest_sems)
    high, low = halves(load_faces((r0, r1, r2, r3)))
    live = live_of(length, n)
    for part, leave, leave_too in zip(chunks(n), totals, rests):
        added = dot(put[part], high) + dot(put[part], low)
        total[part] = own[part] + added
        leave.start()
        applied = dot(offdiag_columns[part], high) + diag[part] * added
        rest[part] = own_resid[part] - live[part] * applied
        leave_too.start()
    for copy in totals + rests:
        copy.wait()


def call(kernel, outs, args, places, out_places="", scratch=(), flops=0):
    size = lambda a: a.size * a.dtype.itemsize
    kinds = dict(s=pltpu.SMEM, v=pltpu.VMEM, h=pltpu.HBM)
    out_places = out_places or "v" * len(outs)
    return pl.pallas_call(
        kernel,
        out_shape=outs,
        in_specs=[pl.BlockSpec(memory_space=kinds[c]) for c in places],
        out_specs=[pl.BlockSpec(memory_space=kinds[c]) for c in out_places],
        scratch_shapes=list(scratch),
        compiler_params=pltpu.CompilerParams(vmem_limit_bytes=VMEM_LIMIT),
        cost_estimate=pl.CostEstimate(
            flops=flops,
            bytes_accessed=sum(size(a) for a in args) + sum(size(a) for a in outs),
            transcendentals=0,
        ),
    )(*args)


def like(*shape, dtype=F32):
    return jax.ShapeDtypeStruct(shape, dtype)


def swap(array, axis, odd):
    size = lax.axis_size(axis)
    pairs = [(i, ((i + odd) ^ 1) - odd) for i in range(size)]
    return lax.ppermute(array, axis, [(i, j) for i, j in pairs if 0 <= j < size])


def exchange(faces):
    return (
        swap(faces[0], "grid", 0),
        swap(faces[1], "grid", 1),
        swap(faces[2], "sub", 1),
        swap(faces[3], "sub", 0),
    )


def body(
    load_parts,
    iface_len,
    face_rows,
    face_count,
    local_inverse,
    schur_offdiag,
    schur_diag,
    mode_basis,
    coarse_inverse,
):
    loads = load_parts[0]
    inverse = local_inverse[0]
    offdiag = schur_offdiag[0]
    diag = schur_diag[0][:, None]
    basis = mode_basis[0]
    basis_t = basis.T
    n, nloads = loads.shape
    modes = basis.shape[0]
    share = face_rows.shape[2]
    nsub = lax.axis_size("sub")
    ngrid = lax.axis_size("grid")
    core = lax.rem(lax.axis_index("sub"), 2)
    column = lax.rem(lax.axis_index("grid"), 2)

    usable = jnp.arange(share)[None, :] < face_count[0][:, None]
    rows = jnp.where(usable, face_rows[0], -1)
    rows_grid = jnp.where(column == 0, rows[2:], rows[:1:-1])
    rows_sub = jnp.where(core == 0, rows[1::-1], rows[:2])
    rows = jnp.concatenate([rows_grid, rows_sub], axis=0).reshape(-1)
    nrows = rows.shape[0]
    core = core[None]

    face = like(share, nloads)
    block = like(n, nloads)
    gather_flops = 4 * nrows * n * nloads
    square_flops = 2 * n * n * nloads

    order = coarse_inverse.shape
    sems = pltpu.SemaphoreType.DMA((CHUNKS,))
    mark = like(8, 128)
    (put,) = call(put_kernel, [like(n, nrows, dtype=BF16)], (rows[None, :],), "v")
    resid, *sent = call(
        begin_kernel, [block] + [face] * 4, (iface_len, loads, put), "svv", flops=gather_flops
    )
    solution = None
    for sweep in range(ITERS):
        received = exchange(sent)
        assembled, coarse_in, after = call(
            coarse_in_kernel,
            [like(n, nloads, dtype=BF16), like(ngrid, modes, nloads), mark],
            (resid, *received, put, basis),
            "v" * 7,
            flops=gather_flops,
        )
        gathered = lax.all_to_all(coarse_in, "grid", 0, 0)
        if sweep == 0:
            local, local_faces, ahead = call(
                local_kernel,
                [block, like(nrows, nloads), mark],
                (inverse, assembled, put),
                "vvv",
                flops=square_flops + gather_flops,
            )
            offdiag_rows, basis_rows, diag_rows, after = call(
                rows_kernel,
                [like(nrows, n, dtype=BF16), like(nrows, modes, dtype=BF16), like(nrows, 128), mark],
                (after, put, offdiag, basis_t, diag),
                "vvvvv",
                flops=2 * nrows * n * n,
            )
        else:
            ahead = after
        keep, send, after = call(
            coarse_kernel,
            [like(order[0] // 2, nloads)] * 2 + [mark],
            (core, coarse_inverse, gathered, after, ahead),
            "svvvv",
            flops=6 * order[0] * order[1] * nloads,
        )
        other = swap(send, "sub", 0)
        groups = [list(range(i, nsub, 2)) for i in range(2)]
        if sweep == 0:
            parts = (keep + other).reshape(nsub // 2, modes, nloads)
        else:
            local, after = call(
                late_local_kernel, [block, mark], (after, inverse, assembled), "vvv", flops=square_flops
            )
            (parts,) = call(sum_kernel, [like(nsub // 2, modes, nloads)], (keep, other, after), "vvv")
        parts = lax.all_to_all(parts, "sub", 0, 0, axis_index_groups=groups)
        if sweep == 0:
            coarse_out, *corrected = call(
                sent_kernel, [like(modes, nloads)] + [face] * 4, (parts, local_faces, basis_rows), "vvv"
            )
        else:
            coarse_out, *corrected = call(
                late_sent_kernel,
                [like(modes, nloads)] + [face] * 4,
                (parts, local, put, basis_rows),
                "vvvv",
                flops=gather_flops,
            )
        received = exchange(corrected)
        if sweep < ITERS - 1:
            (correction,) = call(
                correction_kernel, [block], (iface_len, local, basis_t, coarse_out), "svvv"
            )
            increment, *sent = call(
                increment_kernel,
                [block] + [face] * 4,
                (correction, *received, put, offdiag_rows, diag_rows, *corrected, *sent),
                "v" * 16,
                flops=2 * gather_flops,
            )
            assert solution is None
            resid, solution, offdiag_columns = call(
                residual_kernel,
                [block, block, like(n, nrows, dtype=BF16)],
                (iface_len, increment, diag, loads, offdiag, put),
                "svvvvv",
                "vhv",
                [pltpu.SemaphoreType.DMA],
                flops=square_flops,
            )
        else:
            own, own_resid = call(
                own_kernel,
                [block, block],
                (iface_len, local, basis_t, coarse_out, solution, diag, resid, offdiag),
                "svvvvvvv",
                flops=square_flops,
            )
            solution, resid = call(
                finish_kernel,
                [block, block],
                (iface_len, *received, put, offdiag_columns, diag, own, own_resid),
                "s" + "v" * 9,
                "hh",
                [pltpu.VMEM((n, nloads), F32)] * 2 + [sems] * 2,
                flops=2 * gather_flops,
            )
    return (solution[None], resid[None])


def solution(mesh):
    in_specs = (
        P(("sub", "grid"), None, None),
        P(("sub", "grid")),
        P(("sub", "grid"), None, None),
        P(("sub", "grid"), None),
        P(("sub", "grid"), None, None),
        P(("sub", "grid"), None, None),
        P(("sub", "grid"), None),
        P(("sub", "grid"), None, None),
        P("grid", "sub"),
    )
    out_specs = (P(("sub", "grid"), None, None), P(("sub", "grid"), None, None))
    return jax.shard_map(body, mesh=mesh, in_specs=in_specs, out_specs=out_specs, check_vma=False)
```

```python
import jax
import jax.numpy as jnp
from jax import lax
from jax.experimental import pallas as pl
from jax.experimental.pallas import tpu as pltpu
from jax.sharding import PartitionSpec as P

ITERS = 2
CHUNKS = 4
VMEM_LIMIT = 32 * 1024 * 1024
F32 = jnp.float32
BF16 = jnp.bfloat16


def dot(a, b):
    return jnp.dot(a, b, preferred_element_type=F32)


def halves(v):
    high = v.astype(BF16)
    return high, (v - high.astype(F32)).astype(BF16)


def dot_t(a, b):
    return lax.dot_general(a, b, (((0,), (0,)), ((), ())), preferred_element_type=F32)


def place(put, v):
    high, low = halves(v)
    return dot(put, high) + dot(put, low)


def take(put, v):
    high, low = halves(v)
    return dot_t(put, high) + dot_t(put, low)


def live_of(length_ref, n):
    return (lax.broadcasted_iota(jnp.int32, (n, 1), 0) < length_ref[0]).astype(F32)


def onehot(rows, shape, axis):
    spot = lax.broadcasted_iota(jnp.int32, shape, axis)
    return (rows == spot).astype(F32).astype(BF16)


def store_faces(faces, refs):
    share = refs[0].shape[0]
    for j, ref in enumerate(refs):
        ref[...] = faces[j * share : (j + 1) * share]


def load_faces(refs):
    return jnp.concatenate([ref[...] for ref in refs], axis=0)


def chunks(n):
    return [slice(j * (n // CHUNKS), (j + 1) * (n // CHUNKS)) for j in range(CHUNKS)]


def chunk_copies(source, target, sems):
    return [
        pltpu.make_async_copy(source.at[part], target.at[part], sems.at[j])
        for j, part in enumerate(chunks(target.shape[0]))
    ]


def put_kernel(rows, put):
    put[...] = onehot(rows[...], put.shape, 0)


def begin_kernel(length, loads, put, resid, f0, f1, f2, f3):
    resid[...] = loads[...] * live_of(length, resid.shape[0])
    store_faces(take(put[...], resid[...]), (f0, f1, f2, f3))


def coarse_in_kernel(resid, f0, f1, f2, f3, put, basis, assembled, coarse_in, token):
    token[...] = jnp.zeros_like(token)
    received = load_faces((f0, f1, f2, f3))
    assembled[...] = (resid[...] + place(put[...], received)).astype(BF16)
    block = dot(basis[...], assembled[...])
    for j in range(coarse_in.shape[0]):
        coarse_in[j] = block


def local_kernel(inverse, assembled, put, local, local_faces, token):
    local[...] = dot(inverse[...], assembled[...])
    local_faces[...] = take(put[...], local[...])
    token[...] = jnp.zeros_like(token)


def late_local_kernel(after, inverse, assembled, local, token):
    token[...] = after[...]
    local[...] = dot(inverse[...], assembled[...])


def sum_kernel(keep, other, after, out):
    out[...] = (keep[...] + other[...]).reshape(out.shape)


def coarse_kernel(core, coarse, gathered, after, after_too, keep, send, token):
    token[...] = after[...]
    groups, modes, loads = gathered.shape
    g_high, g_low = halves(gathered[...].reshape(groups * modes, loads))
    high, low = halves(coarse[...])
    out = dot(high, g_high) + dot(high, g_low) + dot(low, g_high)
    pairs = out.reshape(-1, 2, modes, loads)
    even = pairs[:, 0].reshape(keep.shape)
    odd = pairs[:, 1].reshape(keep.shape)
    first = core[0] == 0
    keep[...] = jnp.where(first, even, odd)
    send[...] = jnp.where(first, odd, even)


def rows_kernel(after, put, offdiag, basis_t, diag, offdiag_rows, basis_rows, diag_rows, offdiag_shared, token):
    token[...] = after[...]
    basis_rows[...] = dot_t(put[...], basis_t[...]).astype(BF16)
    wide = jnp.broadcast_to(diag[...], (diag.shape[0], 128))
    diag_rows[...] = take(put[...], wide)
    offdiag_rows[...] = dot_t(put[...], offdiag[...]).astype(BF16)
    offdiag_shared[...] = dot(offdiag_rows[...], put[...]).astype(BF16)


def late_sent_kernel(parts, local, put, basis_rows, coarse_out, f0, f1, f2, f3):
    total = jnp.sum(parts[...], axis=0)
    coarse_out[...] = total
    high, low = halves(total)
    rows = basis_rows[...]
    store_faces(take(put[...], local[...]) + dot(rows, high) + dot(rows, low), (f0, f1, f2, f3))


def sent_kernel(parts, local_faces, basis_rows, coarse_out, f0, f1, f2, f3):
    total = jnp.sum(parts[...], axis=0)
    coarse_out[...] = total
    high, low = halves(total)
    rows = basis_rows[...]
    store_faces(local_faces[...] + dot(rows, high) + dot(rows, low), (f0, f1, f2, f3))


def correct(length, local, basis_t, coarse_out):
    high, low = halves(coarse_out[...])
    spread = dot(basis_t[...], high) + dot(basis_t[...], low)
    return live_of(length, local.shape[0]) * (local[...] + spread)


def correction_kernel(length, local, basis_t, coarse_out, offdiag_rows, correction, applied_rows):
    correction[...] = correct(length, local, basis_t, coarse_out)
    applied_rows[...] = dot(offdiag_rows[...], correction[...].astype(BF16))


def faces_kernel(applied_rows, r0, r1, r2, r3, offdiag_shared, diag_rows, c0, c1, c2, c3, p0, p1, p2, p3,
                 g0, g1, g2, g3, token):
    token[...] = jnp.zeros_like(token)
    received = load_faces((r0, r1, r2, r3))
    there = load_faces((c0, c1, c2, c3)) + received
    applied = applied_rows[...] + dot(offdiag_shared[...], received.astype(BF16)) + diag_rows[:, :1] * there
    store_faces(load_faces((p0, p1, p2, p3)) - applied, (g0, g1, g2, g3))


def residual_kernel(after, length, correction, r0, r1, r2, r3, diag, loads, offdiag, put,
                    resid_out, solution, offdiag_columns, increment, sem):
    increment[...] = correction[...] + place(put[...], load_faces((r0, r1, r2, r3)))
    leave = pltpu.make_async_copy(increment, solution, sem)
    leave.start()
    applied = dot(offdiag[...], increment[...].astype(BF16)) + diag[...] * increment[...]
    resid_out[...] = (loads[...] - applied) * live_of(length, loads.shape[0])
    offdiag_columns[...] = dot(offdiag[...], put[...]).astype(BF16)
    leave.wait()


def own_kernel(length, local, basis_t, coarse_out, before, diag, resid, offdiag,
               solution, resid_out):
    correction = correct(length, local, basis_t, coarse_out)
    solution[...] = before[...] + correction
    applied = dot(offdiag[...], correction.astype(BF16)) + diag[...] * correction
    resid_out[...] = resid[...] - live_of(length, resid.shape[0]) * applied


def finish_kernel(length, r0, r1, r2, r3, put, offdiag_columns, diag, own, own_resid,
                  solution, resid_out, total, rest, total_sems, rest_sems):
    n = own.shape[0]
    totals = chunk_copies(total, solution, total_sems)
    rests = chunk_copies(rest, resid_out, rest_sems)
    high, low = halves(load_faces((r0, r1, r2, r3)))
    live = live_of(length, n)
    for part, leave, leave_too in zip(chunks(n), totals, rests):
        added = dot(put[part], high) + dot(put[part], low)
        total[part] = own[part] + added
        leave.start()
        applied = dot(offdiag_columns[part], high) + diag[part] * added
        rest[part] = own_resid[part] - live[part] * applied
        leave_too.start()
    for copy in totals + rests:
        copy.wait()


def call(kernel, outs, args, places, out_places="", scratch=(), flops=0):
    size = lambda a: a.size * a.dtype.itemsize
    kinds = dict(s=pltpu.SMEM, v=pltpu.VMEM, h=pltpu.HBM)
    out_places = out_places or "v" * len(outs)
    return pl.pallas_call(
        kernel,
        out_shape=outs,
        in_specs=[pl.BlockSpec(memory_space=kinds[c]) for c in places],
        out_specs=[pl.BlockSpec(memory_space=kinds[c]) for c in out_places],
        scratch_shapes=list(scratch),
        compiler_params=pltpu.CompilerParams(vmem_limit_bytes=VMEM_LIMIT),
        cost_estimate=pl.CostEstimate(
            flops=flops,
            bytes_accessed=sum(size(a) for a in args) + sum(size(a) for a in outs),
            transcendentals=0,
        ),
    )(*args)


def like(*shape, dtype=F32):
    return jax.ShapeDtypeStruct(shape, dtype)


def swap(array, axis, odd):
    size = lax.axis_size(axis)
    pairs = [(i, ((i + odd) ^ 1) - odd) for i in range(size)]
    return lax.ppermute(array, axis, [(i, j) for i, j in pairs if 0 <= j < size])


def exchange(faces):
    return (
        swap(faces[0], "grid", 0),
        swap(faces[1], "grid", 1),
        swap(faces[2], "sub", 1),
        swap(faces[3], "sub", 0),
    )


def body(
    load_parts,
    iface_len,
    face_rows,
    face_count,
    local_inverse,
    schur_offdiag,
    schur_diag,
    mode_basis,
    coarse_inverse,
):
    loads = load_parts[0]
    inverse = local_inverse[0]
    offdiag = schur_offdiag[0]
    diag = schur_diag[0][:, None]
    basis = mode_basis[0]
    basis_t = basis.T
    n, nloads = loads.shape
    modes = basis.shape[0]
    share = face_rows.shape[2]
    nsub = lax.axis_size("sub")
    ngrid = lax.axis_size("grid")
    core = lax.rem(lax.axis_index("sub"), 2)
    column = lax.rem(lax.axis_index("grid"), 2)

    usable = jnp.arange(share)[None, :] < face_count[0][:, None]
    rows = jnp.where(usable, face_rows[0], -1)
    rows_grid = jnp.where(column == 0, rows[2:], rows[:1:-1])
    rows_sub = jnp.where(core == 0, rows[1::-1], rows[:2])
    rows = jnp.concatenate([rows_grid, rows_sub], axis=0).reshape(-1)
    nrows = rows.shape[0]
    core = core[None]

    face = like(share, nloads)
    block = like(n, nloads)
    gather_flops = 4 * nrows * n * nloads
    square_flops = 2 * n * n * nloads

    order = coarse_inverse.shape
    sems = pltpu.SemaphoreType.DMA((CHUNKS,))
    mark = like(8, 128)
    (put,) = call(put_kernel, [like(n, nrows, dtype=BF16)], (rows[None, :],), "v")
    resid, *sent = call(
        begin_kernel, [block] + [face] * 4, (iface_len, loads, put), "svv", flops=gather_flops
    )
    solution = None
    for sweep in range(ITERS):
        received = exchange(sent)
        assembled, coarse_in, after = call(
            coarse_in_kernel,
            [like(n, nloads, dtype=BF16), like(ngrid, modes, nloads), mark],
            (resid, *received, put, basis),
            "v" * 7,
            flops=gather_flops,
        )
        gathered = lax.all_to_all(coarse_in, "grid", 0, 0)
        if sweep == 0:
            local, local_faces, ahead = call(
                local_kernel,
                [block, like(nrows, nloads), mark],
                (inverse, assembled, put),
                "vvv",
                flops=square_flops + gather_flops,
            )
            offdiag_rows, basis_rows, diag_rows, offdiag_shared, after = call(
                rows_kernel,
                [like(nrows, n, dtype=BF16), like(nrows, modes, dtype=BF16), like(nrows, 128),
                 like(nrows, nrows, dtype=BF16), mark],
                (after, put, offdiag, basis_t, diag),
                "vvvvv",
                flops=2 * nrows * n * n,
            )
        else:
            ahead = after
        keep, send, after = call(
            coarse_kernel,
            [like(order[0] // 2, nloads)] * 2 + [mark],
            (core, coarse_inverse, gathered, after, ahead),
            "svvvv",
            flops=6 * order[0] * order[1] * nloads,
        )
        other = swap(send, "sub", 0)
        groups = [list(range(i, nsub, 2)) for i in range(2)]
        if sweep == 0:
            parts = (keep + other).reshape(nsub // 2, modes, nloads)
        else:
            local, after = call(
                late_local_kernel, [block, mark], (after, inverse, assembled), "vvv", flops=square_flops
            )
            (parts,) = call(sum_kernel, [like(nsub // 2, modes, nloads)], (keep, other, after), "vvv")
        parts = lax.all_to_all(parts, "sub", 0, 0, axis_index_groups=groups)
        if sweep == 0:
            coarse_out, *corrected = call(
                sent_kernel, [like(modes, nloads)] + [face] * 4, (parts, local_faces, basis_rows), "vvv"
            )
        else:
            coarse_out, *corrected = call(
                late_sent_kernel,
                [like(modes, nloads)] + [face] * 4,
                (parts, local, put, basis_rows),
                "vvvv",
                flops=gather_flops,
            )
        received = exchange(corrected)
        if sweep < ITERS - 1:
            correction, applied_rows = call(
                correction_kernel,
                [block, like(nrows, nloads)],
                (iface_len, local, basis_t, coarse_out, offdiag_rows),
                "svvvv",
                flops=gather_flops // 2,
            )
            *sent, after = call(
                faces_kernel,
                [face] * 4 + [mark],
                (applied_rows, *received, offdiag_shared, diag_rows, *corrected, *sent),
                "v" * 15,
            )
            assert solution is None
            resid, solution, offdiag_columns = call(
                residual_kernel,
                [block, block, like(n, nrows, dtype=BF16)],
                (after, iface_len, correction, *received, diag, loads, offdiag, put),
                "vs" + "v" * 9,
                "vhv",
                [pltpu.VMEM((n, nloads), F32), pltpu.SemaphoreType.DMA],
                flops=square_flops,
            )
        else:
            own, own_resid = call(
                own_kernel,
                [block, block],
                (iface_len, local, basis_t, coarse_out, solution, diag, resid, offdiag),
                "svvvvvvv",
                flops=square_flops,
            )
            solution, resid = call(
                finish_kernel,
                [block, block],
                (iface_len, *received, put, offdiag_columns, diag, own, own_resid),
                "s" + "v" * 9,
                "hh",
                [pltpu.VMEM((n, nloads), F32)] * 2 + [sems] * 2,
                flops=2 * gather_flops,
            )
    return (solution[None], resid[None])


def solution(mesh):
    in_specs = (
        P(("sub", "grid"), None, None),
        P(("sub", "grid")),
        P(("sub", "grid"), None, None),
        P(("sub", "grid"), None),
        P(("sub", "grid"), None, None),
        P(("sub", "grid"), None, None),
        P(("sub", "grid"), None),
        P(("sub", "grid"), None, None),
        P("grid", "sub"),
    )
    out_specs = (P(("sub", "grid"), None, None), P(("sub", "grid"), None, None))
    return jax.shard_map(body, mesh=mesh, in_specs=in_specs, out_specs=out_specs, check_vma=False)
```

```python
import jax
import jax.numpy as jnp
from jax import lax
from jax.experimental import pallas as pl
from jax.experimental.pallas import tpu as pltpu
from jax.sharding import PartitionSpec as P

ITERS = 2
CHUNKS = 4
VMEM_LIMIT = 32 * 1024 * 1024
F32 = jnp.float32
BF16 = jnp.bfloat16


def dot(a, b):
    return jnp.dot(a, b, preferred_element_type=F32)


def halves(v):
    high = v.astype(BF16)
    return high, (v - high.astype(F32)).astype(BF16)


def dot_t(a, b):
    return lax.dot_general(a, b, (((0,), (0,)), ((), ())), preferred_element_type=F32)


def place(put, v):
    high, low = halves(v)
    return dot(put, high) + dot(put, low)


def take(put, v):
    high, low = halves(v)
    return dot_t(put, high) + dot_t(put, low)


def live_of(length_ref, n):
    return (lax.broadcasted_iota(jnp.int32, (n, 1), 0) < length_ref[0]).astype(F32)


def onehot(rows, shape, axis):
    spot = lax.broadcasted_iota(jnp.int32, shape, axis)
    return (rows == spot).astype(F32).astype(BF16)


def store_faces(faces, refs):
    share = refs[0].shape[0]
    for j, ref in enumerate(refs):
        ref[...] = faces[j * share : (j + 1) * share]


def load_faces(refs):
    return jnp.concatenate([ref[...] for ref in refs], axis=0)


def chunks(n):
    return [slice(j * (n // CHUNKS), (j + 1) * (n // CHUNKS)) for j in range(CHUNKS)]


def chunk_copies(source, target, sems):
    return [
        pltpu.make_async_copy(source.at[part], target.at[part], sems.at[j])
        for j, part in enumerate(chunks(target.shape[0]))
    ]


def put_kernel(rows, put):
    put[...] = onehot(rows[...], put.shape, 0)


def begin_kernel(length, loads, put, resid, f0, f1, f2, f3):
    resid[...] = loads[...] * live_of(length, resid.shape[0])
    store_faces(take(put[...], resid[...]), (f0, f1, f2, f3))


def coarse_in_kernel(resid, f0, f1, f2, f3, put, basis, assembled, coarse_in, token):
    token[...] = jnp.zeros_like(token)
    received = load_faces((f0, f1, f2, f3))
    assembled[...] = (resid[...] + place(put[...], received)).astype(BF16)
    block = dot(basis[...], assembled[...])
    for j in range(coarse_in.shape[0]):
        coarse_in[j] = block


def local_kernel(inverse, assembled, put, local, local_faces, token):
    local[...] = dot(inverse[...], assembled[...])
    local_faces[...] = take(put[...], local[...])
    token[...] = jnp.zeros_like(token)


def late_local_kernel(after, inverse, assembled, local, token):
    token[...] = after[...]
    local[...] = dot(inverse[...], assembled[...])


def sum_kernel(keep, other, after, out):
    out[...] = (keep[...] + other[...]).reshape(out.shape)


def coarse_kernel(core, coarse, gathered, after, after_too, keep, send, token):
    token[...] = after[...]
    groups, modes, loads = gathered.shape
    g_high, g_low = halves(gathered[...].reshape(groups * modes, loads))
    high, low = halves(coarse[...])
    out = dot(high, g_high) + dot(high, g_low) + dot(low, g_high)
    pairs = out.reshape(-1, 2, modes, loads)
    even = pairs[:, 0].reshape(keep.shape)
    odd = pairs[:, 1].reshape(keep.shape)
    first = core[0] == 0
    keep[...] = jnp.where(first, even, odd)
    send[...] = jnp.where(first, odd, even)


def rows_kernel(after, put, offdiag, basis_t, diag, offdiag_rows, basis_rows, diag_rows, offdiag_shared, token):
    token[...] = after[...]
    basis_rows[...] = dot_t(put[...], basis_t[...]).astype(BF16)
    wide = jnp.broadcast_to(diag[...], (diag.shape[0], 128))
    diag_rows[...] = take(put[...], wide)
    offdiag_rows[...] = dot_t(put[...], offdiag[...]).astype(BF16)
    offdiag_shared[...] = dot(offdiag_rows[...], put[...]).astype(BF16)


def late_sent_kernel(parts, local, put, basis_rows, coarse_out, f0, f1, f2, f3):
    total = jnp.sum(parts[...], axis=0)
    coarse_out[...] = total
    high, low = halves(total)
    rows = basis_rows[...]
    store_faces(take(put[...], local[...]) + dot(rows, high) + dot(rows, low), (f0, f1, f2, f3))


def sent_kernel(parts, local_faces, basis_rows, coarse_out, f0, f1, f2, f3):
    total = jnp.sum(parts[...], axis=0)
    coarse_out[...] = total
    high, low = halves(total)
    rows = basis_rows[...]
    store_faces(local_faces[...] + dot(rows, high) + dot(rows, low), (f0, f1, f2, f3))


def correct(length, local, basis_t, coarse_out):
    high, low = halves(coarse_out[...])
    spread = dot(basis_t[...], high) + dot(basis_t[...], low)
    return live_of(length, local.shape[0]) * (local[...] + spread)


def correction_kernel(length, local, basis_t, coarse_out, offdiag_rows, correction, applied_rows):
    correction[...] = correct(length, local, basis_t, coarse_out)
    applied_rows[...] = dot(offdiag_rows[...], correction[...].astype(BF16))


def faces_kernel(applied_rows, r0, r1, r2, r3, offdiag_shared, diag_rows, c0, c1, c2, c3, p0, p1, p2, p3,
                 g0, g1, g2, g3, token):
    token[...] = jnp.zeros_like(token)
    received = load_faces((r0, r1, r2, r3))
    there = load_faces((c0, c1, c2, c3)) + received
    applied = applied_rows[...] + dot(offdiag_shared[...], received.astype(BF16)) + diag_rows[:, :1] * there
    store_faces(load_faces((p0, p1, p2, p3)) - applied, (g0, g1, g2, g3))


def residual_kernel(after, length, correction, r0, r1, r2, r3, diag, loads, offdiag, put,
                    resid_out, solution, increment, sem):
    increment[...] = correction[...] + place(put[...], load_faces((r0, r1, r2, r3)))
    leave = pltpu.make_async_copy(increment, solution, sem)
    leave.start()
    applied = dot(offdiag[...], increment[...].astype(BF16)) + diag[...] * increment[...]
    resid_out[...] = (loads[...] - applied) * live_of(length, loads.shape[0])
    leave.wait()


def own_kernel(length, local, basis_t, coarse_out, before, diag, resid, offdiag, put,
               solution, resid_out, offdiag_columns):
    correction = correct(length, local, basis_t, coarse_out)
    solution[...] = before[...] + correction
    applied = dot(offdiag[...], correction.astype(BF16)) + diag[...] * correction
    resid_out[...] = resid[...] - live_of(length, resid.shape[0]) * applied
    offdiag_columns[...] = dot(offdiag[...], put[...]).astype(BF16)


def finish_kernel(length, r0, r1, r2, r3, put, offdiag_columns, diag, own, own_resid,
                  solution, resid_out, total, rest, total_sems, rest_sems):
    n = own.shape[0]
    totals = chunk_copies(total, solution, total_sems)
    rests = chunk_copies(rest, resid_out, rest_sems)
    high, low = halves(load_faces((r0, r1, r2, r3)))
    live = live_of(length, n)
    for part, leave, leave_too in zip(chunks(n), totals, rests):
        added = dot(put[part], high) + dot(put[part], low)
        total[part] = own[part] + added
        leave.start()
        applied = dot(offdiag_columns[part], high) + diag[part] * added
        rest[part] = own_resid[part] - live[part] * applied
        leave_too.start()
    for copy in totals + rests:
        copy.wait()


def call(kernel, outs, args, places, out_places="", scratch=(), flops=0):
    size = lambda a: a.size * a.dtype.itemsize
    kinds = dict(s=pltpu.SMEM, v=pltpu.VMEM, h=pltpu.HBM)
    out_places = out_places or "v" * len(outs)
    return pl.pallas_call(
        kernel,
        out_shape=outs,
        in_specs=[pl.BlockSpec(memory_space=kinds[c]) for c in places],
        out_specs=[pl.BlockSpec(memory_space=kinds[c]) for c in out_places],
        scratch_shapes=list(scratch),
        compiler_params=pltpu.CompilerParams(vmem_limit_bytes=VMEM_LIMIT),
        cost_estimate=pl.CostEstimate(
            flops=flops,
            bytes_accessed=sum(size(a) for a in args) + sum(size(a) for a in outs),
            transcendentals=0,
        ),
    )(*args)


def like(*shape, dtype=F32):
    return jax.ShapeDtypeStruct(shape, dtype)


def swap(array, axis, odd):
    size = lax.axis_size(axis)
    pairs = [(i, ((i + odd) ^ 1) - odd) for i in range(size)]
    return lax.ppermute(array, axis, [(i, j) for i, j in pairs if 0 <= j < size])


def exchange(faces):
    return (
        swap(faces[0], "grid", 0),
        swap(faces[1], "grid", 1),
        swap(faces[2], "sub", 1),
        swap(faces[3], "sub", 0),
    )


def body(
    load_parts,
    iface_len,
    face_rows,
    face_count,
    local_inverse,
    schur_offdiag,
    schur_diag,
    mode_basis,
    coarse_inverse,
):
    loads = load_parts[0]
    inverse = local_inverse[0]
    offdiag = schur_offdiag[0]
    diag = schur_diag[0][:, None]
    basis = mode_basis[0]
    basis_t = basis.T
    n, nloads = loads.shape
    modes = basis.shape[0]
    share = face_rows.shape[2]
    nsub = lax.axis_size("sub")
    ngrid = lax.axis_size("grid")
    core = lax.rem(lax.axis_index("sub"), 2)
    column = lax.rem(lax.axis_index("grid"), 2)

    usable = jnp.arange(share)[None, :] < face_count[0][:, None]
    rows = jnp.where(usable, face_rows[0], -1)
    rows_grid = jnp.where(column == 0, rows[2:], rows[:1:-1])
    rows_sub = jnp.where(core == 0, rows[1::-1], rows[:2])
    rows = jnp.concatenate([rows_grid, rows_sub], axis=0).reshape(-1)
    nrows = rows.shape[0]
    core = core[None]

    face = like(share, nloads)
    block = like(n, nloads)
    gather_flops = 4 * nrows * n * nloads
    square_flops = 2 * n * n * nloads

    order = coarse_inverse.shape
    sems = pltpu.SemaphoreType.DMA((CHUNKS,))
    mark = like(8, 128)
    (put,) = call(put_kernel, [like(n, nrows, dtype=BF16)], (rows[None, :],), "v")
    resid, *sent = call(
        begin_kernel, [block] + [face] * 4, (iface_len, loads, put), "svv", flops=gather_flops
    )
    solution = None
    for sweep in range(ITERS):
        received = exchange(sent)
        assembled, coarse_in, after = call(
            coarse_in_kernel,
            [like(n, nloads, dtype=BF16), like(ngrid, modes, nloads), mark],
            (resid, *received, put, basis),
            "v" * 7,
            flops=gather_flops,
        )
        gathered = lax.all_to_all(coarse_in, "grid", 0, 0)
        if sweep == 0:
            local, local_faces, ahead = call(
                local_kernel,
                [block, like(nrows, nloads), mark],
                (inverse, assembled, put),
                "vvv",
                flops=square_flops + gather_flops,
            )
            offdiag_rows, basis_rows, diag_rows, offdiag_shared, after = call(
                rows_kernel,
                [like(nrows, n, dtype=BF16), like(nrows, modes, dtype=BF16), like(nrows, 128),
                 like(nrows, nrows, dtype=BF16), mark],
                (after, put, offdiag, basis_t, diag),
                "vvvvv",
                flops=2 * nrows * n * n,
            )
        else:
            ahead = after
        keep, send, after = call(
            coarse_kernel,
            [like(order[0] // 2, nloads)] * 2 + [mark],
            (core, coarse_inverse, gathered, after, ahead),
            "svvvv",
            flops=6 * order[0] * order[1] * nloads,
        )
        other = swap(send, "sub", 0)
        groups = [list(range(i, nsub, 2)) for i in range(2)]
        if sweep == 0:
            parts = (keep + other).reshape(nsub // 2, modes, nloads)
        else:
            local, after = call(
                late_local_kernel, [block, mark], (after, inverse, assembled), "vvv", flops=square_flops
            )
            (parts,) = call(sum_kernel, [like(nsub // 2, modes, nloads)], (keep, other, after), "vvv")
        parts = lax.all_to_all(parts, "sub", 0, 0, axis_index_groups=groups)
        if sweep == 0:
            coarse_out, *corrected = call(
                sent_kernel, [like(modes, nloads)] + [face] * 4, (parts, local_faces, basis_rows), "vvv"
            )
        else:
            coarse_out, *corrected = call(
                late_sent_kernel,
                [like(modes, nloads)] + [face] * 4,
                (parts, local, put, basis_rows),
                "vvvv",
                flops=gather_flops,
            )
        received = exchange(corrected)
        if sweep < ITERS - 1:
            correction, applied_rows = call(
                correction_kernel,
                [block, like(nrows, nloads)],
                (iface_len, local, basis_t, coarse_out, offdiag_rows),
                "svvvv",
                flops=gather_flops // 2,
            )
            *sent, after = call(
                faces_kernel,
                [face] * 4 + [mark],
                (applied_rows, *received, offdiag_shared, diag_rows, *corrected, *sent),
                "v" * 15,
            )
            assert solution is None
            resid, solution = call(
                residual_kernel,
                [block, block],
                (after, iface_len, correction, *received, diag, loads, offdiag, put),
                "vs" + "v" * 9,
                "vh",
                [pltpu.VMEM((n, nloads), F32), pltpu.SemaphoreType.DMA],
                flops=square_flops,
            )
        else:
            own, own_resid, offdiag_columns = call(
                own_kernel,
                [block, block, like(n, nrows, dtype=BF16)],
                (iface_len, local, basis_t, coarse_out, solution, diag, resid, offdiag, put),
                "svvvvvvvv",
                flops=square_flops,
            )
            solution, resid = call(
                finish_kernel,
                [block, block],
                (iface_len, *received, put, offdiag_columns, diag, own, own_resid),
                "s" + "v" * 9,
                "hh",
                [pltpu.VMEM((n, nloads), F32)] * 2 + [sems] * 2,
                flops=2 * gather_flops,
            )
    return (solution[None], resid[None])


def solution(mesh):
    in_specs = (
        P(("sub", "grid"), None, None),
        P(("sub", "grid")),
        P(("sub", "grid"), None, None),
        P(("sub", "grid"), None),
        P(("sub", "grid"), None, None),
        P(("sub", "grid"), None, None),
        P(("sub", "grid"), None),
        P(("sub", "grid"), None, None),
        P("grid", "sub"),
    )
    out_specs = (P(("sub", "grid"), None, None), P(("sub", "grid"), None, None))
    return jax.shard_map(body, mesh=mesh, in_specs=in_specs, out_specs=out_specs, check_vma=False)
```
